256 devices in a mesh: src: 2 (over x_lo), lat: 128 (over z, x_hi, y, core).
Axes of the slice: x: 4 (x_hi: 2, x_lo: 2; x = x_hi * 2 + x_lo), y: 4, z: 8, core: 2. Of those that a mesh axis runs over, the one named last changes fastest.
Arguments:
- resid: bfloat16 [2, 512, 4096], P('src', 'lat'), may hold values from -6 to 6
- token_ids: int32 [512], replicated, may hold values from 0 to 511, each once
- enc_weight: bfloat16 [2, 4096, 32768], P('src', None, 'lat'), may hold values from -0.09375 to 0.09375
- enc_bias: float32 [2, 32768], P('src', 'lat'), may hold values from -3.2 to -1.8
- threshold: float32 [2, 32768], P('src', 'lat'), may hold values from 0.1 to 1
- dec_self: bfloat16 [2, 32768, 4096], P('src', 'lat'), may hold values from -0.375 to 0.375
- dec_cross: bfloat16 [32768, 4096], P('lat'), may hold values from -0.375 to 0.375
Outputs:
- recon: bfloat16 [2, 512, 4096], P('src', 'lat')
The draws below stay inside these ranges and needn't reach their ends.
Inputs may be any that keep to these rules, and one draw needn't show every extreme that they name: token_ids names every pool row exactly once.
All inputs are finite; a program needn't handle non-finite values.
Results may differ from the reference program's by a relative error of at most 0.005.
Values may be sent and summed in bfloat16 or wider, within the bound.
A program may use at most 128 MiB of HBM per device.

```python
import math
import jax
import jax.numpy as jnp

D = 4096
LATENTS = 32768
TOKENS = 512


def shard_levels(key, extent, split, low, top_value):
    factor_of = 1.0
    for axis_at, parts in split:
        steps = jax.random.uniform(jax.random.fold_in(jax.random.fold_in(key, 6), axis_at), (parts,), jnp.float32, low / len(split), top_value / len(split))
        factor_of = factor_of * jnp.repeat(jnp.exp(steps), extent[axis_at] // parts).reshape((-1,) + (1,) * (len(extent) - 1 - axis_at))
    return factor_of


def bell_draw(stream_key, dims, scale, bound, split=(), kind=jnp.bfloat16):
    factor_of = shard_levels(stream_key, dims, split, -0.22, 0.18) if split else 1.0
    array = jax.random.normal(stream_key, dims, jnp.float32) * scale * factor_of
    return jnp.minimum(jnp.maximum(array, -bound), bound).astype(kind)


def setup_inputs(seed: int = 0) -> dict:
    key_list = jax.random.split(jax.random.key(seed), 8)
    return {
        "resid": bell_draw(key_list[0], (2, TOKENS, D), 1.0, 6.0, ((0, 2), (1, 128))),
        "token_ids": jax.random.permutation(key_list[1], TOKENS).astype(jnp.int32),
        "enc_weight": bell_draw(key_list[2], (2, D, LATENTS), D ** -0.5, 0.09375, ((0, 2), (2, 128))),
        "enc_bias": jnp.clip(-3.2 + 1.4000001 * jax.random.uniform(key_list[3], (2, LATENTS), jnp.float32) ** shard_levels(key_list[3], (2, LATENTS), ((0, 2), (1, 128)), -0.2, 0.2), -3.2, -1.8),
        "threshold": jnp.clip(jnp.exp(math.log(1.0) - 2.3025851 * jax.random.uniform(key_list[4], (2, LATENTS), jnp.float32) ** shard_levels(key_list[4], (2, LATENTS), ((0, 2), (1, 128)), -0.2, 0.2)), 0.1, 1.0),
        "dec_self": bell_draw(key_list[5], (2, LATENTS, D), (max(LATENTS // 128, 1)) ** -0.5, 0.375, ((0, 2), (1, 128))),
        "dec_cross": bell_draw(key_list[6], (LATENTS, D), (max(LATENTS // 128, 1)) ** -0.5, 0.375, ((0, 128),)),
    }


def encode(rows, weight, bias, thresh):
    pre = jnp.dot(rows, weight, preferred_element_type=jnp.float32) + bias
    return (pre * jnp.clip((pre - thresh) / 0.1, 0.0, 1.0)).astype(jnp.bfloat16)


def reference(resid, token_ids, enc_weight, enc_bias, threshold, dec_self, dec_cross):
    selected = jnp.take(resid, token_ids, axis=1)
    first = encode(selected[0], enc_weight[0], enc_bias[0], threshold[0])
    second = encode(selected[1], enc_weight[1], enc_bias[1], threshold[1])
    lower = jnp.dot(first, dec_self[0], preferred_element_type=jnp.float32)
    upper = jnp.dot(second, dec_self[1], preferred_element_type=jnp.float32)
    upper = upper + jnp.dot(first, dec_cross, preferred_element_type=jnp.float32)
    return jnp.stack([lower, upper]).astype(jnp.bfloat16)
```

```python
import jax
import jax.numpy as jnp
from jax import lax
from jax.experimental import pallas as pl
from jax.experimental.pallas import tpu as pltpu
from jax.sharding import PartitionSpec as P

MESH = pl.DeviceIdType.MESH
BF16, F32 = jnp.bfloat16, jnp.float32

NZ, NX, NY = 8, 2, 4
ROWS = 4
D, LAT = 4096, 256
PLANE = NZ * NX * NY * ROWS
QUARTER = D // 4
XFIRST = 384
TILE = 512
TILES = D // TILE
Y_TILES = (0, 3, 6)
Z_GROUPS = ((0, 2), (2, 4), (4, 6), (6, 8))
Z_ORDER = (0, 1, 7, 2, 6, 3, 5, 4)


def kernel(
    ids,
    resid,
    bias,
    thresh,
    enc_hbm,
    own_hbm,
    cross_hbm,
    out,
    blocks,
    rows,
    enc,
    own_dec,
    cross_dec,
    bias2,
    thresh2,
    codes,
    earlier,
    select,
    mixed,
    mixed_cross,
    part,
    send1,
    half,
    send2,
    send3,
    last,
    got_x1,
    got_y2,
    got_y1,
    got_x2,
    got_z,
    local_sem,
    core_send,
    core_recv,
    code_send,
    code_recv,
    z_send,
    z_recv,
    cy_send,
    cy_recv,
    cx_send,
    cx_recv,
    bx_send,
    bx_recv,
    by_send,
    by_recv,
    s1_send,
    s1_recv,
    s2_send,
    s2_recv,
    s3_send,
    s3_recv,
):
    src = lax.axis_index("src")
    lat = lax.axis_index("lat")
    core = lax.rem(lat, 2)
    y = lax.rem(lat // 2, NY)
    x = lax.rem(lat // (2 * NY), NX)
    z = lat // (2 * NY * NX)

    def at(z, x, y, core):
        return (src, ((z * NX + x) * NY + y) * 2 + core)

    def zp(dz):
        return lax.rem(z + NZ - dz, NZ)

    def zn(dz):
        return lax.rem(z + dz, NZ)

    def yn(dy):
        return lax.rem(y + dy, NY)

    other_core = at(z, x, y, 1 - core)
    other_src = (1 - src, lat)
    other_x = at(z, 1 - x, y, core)

    def remote(src_ref, dst_ref, send, recv, device):
        return pltpu.make_async_remote_copy(
            src_ref=src_ref,
            dst_ref=dst_ref,
            send_sem=send,
            recv_sem=recv,
            device_id=device,
            device_id_type=MESH,
        )

    started = []

    def go(copy):
        copy.start()
        started.append(copy)

    locals_ = [
        pltpu.make_async_copy(enc_hbm.at[0], enc.at[core], local_sem.at[0]),
        pltpu.make_async_copy(own_hbm.at[0], own_dec.at[core], local_sem.at[1]),
        pltpu.make_async_copy(cross_hbm, cross_dec.at[core], local_sem.at[2]),
    ]
    for copy in locals_:
        copy.start()

    mine = resid[0].astype(F32)
    blocks[z, x, y] = jnp.concatenate(
        [mine[:, q * QUARTER : (q + 1) * QUARTER] for q in range(4)], axis=0
    ).astype(BF16)

    bias2[core] = bias[...]
    thresh2[core] = thresh[...]

    barrier = pltpu.get_barrier_semaphore()
    peers = [at(zn(o), x, y, core) for o in range(1, NZ)]
    peers += [at(z, x, yn(o), core) for o in range(1, NY)]
    peers += [other_x, other_core, other_src]
    for peer in peers:
        pl.semaphore_signal(barrier, inc=1, device_id=peer, device_id_type=MESH)
    pl.semaphore_wait(barrier, len(peers))

    def z_copy(o):
        ref = blocks.at[z, x, y]
        return remote(ref, ref, z_send.at[o], z_recv.at[o], at(zn(o), x, y, core))

    for o in Z_ORDER[1:]:
        go(z_copy(o))

    b_cols, c_cols = pl.ds(0, XFIRST), pl.ds(XFIRST, QUARTER - XFIRST)

    def cy_copy(dz, o):
        ref = blocks.at[zp(dz), x, y, :, c_cols]
        return remote(
            ref, ref, cy_send.at[dz, o], cy_recv.at[dz, o], at(z, x, yn(o), core)
        )

    def bx_copy(dz):
        ref = blocks.at[zp(dz), x, y, :, b_cols]
        return remote(ref, ref, bx_send.at[dz], bx_recv.at[dz], other_x)

    def cx_copy(dz):
        ref = blocks.at[zp(dz), x, :, :, c_cols]
        return remote(ref, ref, cx_send.at[dz], cx_recv.at[dz], other_x)

    def by_copy(dz, o):
        ref = blocks.at[zp(dz), :, y, :, b_cols]
        return remote(
            ref, ref, by_send.at[dz, o], by_recv.at[dz, o], at(z, x, yn(o), core)
        )

    def second(dz):
        if dz:
            z_copy(dz).wait_recv()
        for o in (1, 3, 2):
            go(cy_copy(dz, o))
        go(bx_copy(dz))

    def third(dz):
        bx_copy(dz).wait_recv()
        for o in (1, 3, 2):
            go(by_copy(dz, o))
        for o in (1, 3, 2):
            cy_copy(dz, o).wait_recv()
        go(cx_copy(dz))

    second(0)

    core_copies = [
        remote(bias, bias2.at[core], core_send.at[3], core_recv.at[3], other_core),
        remote(
            thresh, thresh2.at[core], core_send.at[4], core_recv.at[4], other_core
        ),
        remote(
            enc_hbm.at[0], enc.at[core], core_send.at[0], core_recv.at[0], other_core
        ),
        remote(
            own_hbm.at[0],
            own_dec.at[core],
            core_send.at[1],
            core_recv.at[1],
            other_core,
        ),
    ]
    for copy in core_copies:
        go(copy)
    cross_copy = remote(
        cross_hbm, cross_dec.at[core], core_send.at[2], core_recv.at[2], other_core
    )

    @pl.when(src == 1)
    def _():
        cross_copy.start()

    shape = (2 * PLANE, 2 * PLANE)
    j = lax.broadcasted_iota(jnp.int32, shape, 0)
    plane, within = j // PLANE, j % PLANE
    pool = (within // ROWS) * (2 * ROWS) + plane * ROWS + within % ROWS
    named = (jnp.broadcast_to(ids[...], shape) == pool).astype(F32).astype(BF16)
    i = lax.broadcasted_iota(jnp.int32, (PLANE, 2 * PLANE), 0)
    t = lax.broadcasted_iota(jnp.int32, (PLANE, 2 * PLANE), 1)
    ir, iz, iy, ix = i % 4, (i // 4) % NZ, (i // (4 * NZ)) % NY, i // (4 * NZ * NY)
    token = (((iz * NX + ix) * NY + iy) * 2 + core) * ROWS + ir
    order = (t == token).astype(F32).astype(BF16)
    select[...] = lax.dot_general(
        order, named, (((1,), (1,)), ((), ())), preferred_element_type=F32
    ).astype(BF16)

    lag = 2
    for n, dz in enumerate(Z_ORDER):
        if n:
            second(dz)
        if n >= lag:
            third(Z_ORDER[n - lag])
    for dz in Z_ORDER[NZ - lag :]:
        third(dz)

    def unpack(dz):
        zz = zp(dz)
        for xx in range(NX):
            four = [blocks[zz, xx, yy].astype(F32) for yy in range(NY)]
            start = pl.multiple_of((zz * NX + xx) * (NY * ROWS), NY * ROWS)
            for q in range(4):
                rows[pl.ds(start, NY * ROWS), q * QUARTER : (q + 1) * QUARTER] = (
                    jnp.concatenate([b[4 * q : 4 * q + 4] for b in four], axis=0)
                ).astype(BF16)

    for dz in Z_ORDER:
        for o in (1, 3, 2):
            by_copy(dz, o).wait_recv()
        cx_copy(dz).wait_recv()
        unpack(dz)

    locals_[0].wait()
    for copy in core_copies[:3]:
        copy.wait_recv()
    for h in range(2):
        pre = jnp.dot(rows[...], enc[h], preferred_element_type=F32) + bias2[h]
        gate = jnp.clip((pre - thresh2[h]) / 0.1, 0.0, 1.0)
        codes[core, :, h * LAT : (h + 1) * LAT] = (pre * gate).astype(BF16)

    code_copy = remote(
        codes.at[core], codes.at[core], code_send.at[0], code_recv.at[0], other_core
    )
    go(code_copy)
    over = remote(
        codes.at[core], earlier.at[core], code_send.at[1], code_recv.at[1], other_src
    )
    on = remote(
        earlier.at[core], earlier.at[core], code_send.at[2], code_recv.at[2], other_core
    )

    @pl.when(src == 0)
    def _():
        over.start()

    code_copy.wait_recv()

    def permuted(ref):
        return jnp.dot(
            select[...], ref[...].reshape(2 * PLANE, 2 * LAT), preferred_element_type=F32
        ).astype(BF16)

    mixed[...] = permuted(codes)
    locals_[1].wait()
    core_copies[3].wait_recv()
    locals_[2].wait()

    @pl.when(src == 1)
    def _():
        over.wait_recv()
        on.start()
        cross_copy.wait_recv()
        on.wait_recv()
        mixed_cross[...] = permuted(earlier)

    def decode(n):
        cols = slice(n * TILE, (n + 1) * TILE)
        total = jnp.zeros((PLANE, TILE), F32)
        for h in range(2):
            total += jnp.dot(
                mixed[:, h * LAT : (h + 1) * LAT],
                own_dec[h, :, cols],
                preferred_element_type=F32,
            )
        part[n] = total.reshape(NX, NY, NZ * ROWS, TILE)

        @pl.when(src == 1)
        def _():
            total = part[n].reshape(PLANE, TILE)
            for h in range(2):
                total += jnp.dot(
                    mixed_cross[:, h * LAT : (h + 1) * LAT],
                    cross_dec[h, :, cols],
                    preferred_element_type=F32,
                )
            part[n] = total.reshape(NX, NY, NZ * ROWS, TILE)

        send1[n] = part[n].astype(BF16)

    def y1_copy(n, o):
        return remote(
            send1.at[n, :, yn(o)],
            got_y1.at[n, o],
            s1_send.at[n, o],
            s1_recv.at[n, o],
            at(z, x, yn(o), core),
        )

    def x1_copy(n):
        return remote(
            send1.at[n, 1 - x], got_x1.at[n], s1_send.at[n, 0], s1_recv.at[n, 0], other_x
        )

    def y2_copy(n, o):
        return remote(
            send2.at[n, yn(o)],
            got_y2.at[n, o],
            s2_send.at[n, o],
            s2_recv.at[n, o],
            at(z, x, yn(o), core),
        )

    def x2_copy(n):
        return remote(
            send2.at[n, 1 - x], got_x2.at[n], s2_send.at[n, 0], s2_recv.at[n, 0], other_x
        )

    def z3_copy(g, o):
        first, end = Z_GROUPS[g]
        return remote(
            send3.at[zn(o), pl.ds(first, end - first)],
            got_z.at[o, pl.ds(first, end - first)],
            s3_send.at[g, o],
            s3_recv.at[g, o],
            at(zn(o), x, y, core),
        )

    def stage1(n):
        decode(n)
        if n in Y_TILES:
            for o in (1, 3, 2):
                go(y1_copy(n, o))
        else:
            go(x1_copy(n))

    def stage2(n):
        if n in Y_TILES:
            for o in (1, 3, 2):
                y1_copy(n, o).wait_recv()
            total = part[n, :, y]
            for o in (1, 3, 2):
                total += got_y1[n, o].astype(F32)
            half[n, 0:NX] = total
            send2[n, 0:NX] = total.astype(BF16)
            go(x2_copy(n))
        else:
            x1_copy(n).wait_recv()
            total = part[n, x] + got_x1[n].astype(F32)
            half[n] = total
            send2[n] = total.astype(BF16)
            for o in (1, 3, 2):
                go(y2_copy(n, o))

    def stage3(n):
        if n in Y_TILES:
            x2_copy(n).wait_recv()
            total = half[n, x] + got_x2[n].astype(F32)
        else:
            for o in (1, 3, 2):
                y2_copy(n, o).wait_recv()
            total = half[n, y]
            for o in (1, 3, 2):
                total += got_y2[n, o].astype(F32)
        step = TILE // 4
        for zz in range(NZ):
            block = jnp.concatenate(
                [
                    total[zz * ROWS : (zz + 1) * ROWS, q * step : (q + 1) * step]
                    for q in range(4)
                ],
                axis=0,
            )
            last[zz, n] = block
            send3[zz, n] = block.astype(BF16)
        for g, (_, end) in enumerate(Z_GROUPS):
            if n == end - 1:
                for o in Z_ORDER[:0:-1]:
                    go(z3_copy(g, o))

    def finish(g):
        first, end = Z_GROUPS[g]
        for o in range(1, NZ):
            z3_copy(g, o).wait_recv()
        step = TILE // 4
        for n in range(first, end):
            total = last[z, n]
            for o in range(1, NZ):
                total += got_z[o, n].astype(F32)
            for q in range(4):
                out[0, :, n * TILE + q * step : n * TILE + (q + 1) * step] = total[
                    q * ROWS : (q + 1) * ROWS
                ].astype(BF16)

    for n in range(TILES):
        stage1(n)
    for n in range(TILES + 2):
        if n < TILES:
            stage2(n)
        if n >= 2:
            stage3(n - 2)
    for g in range(len(Z_GROUPS)):
        finish(g)

    for copy in started:
        copy.wait_send()

    @pl.when(src == 0)
    def _():
        over.wait_send()

    @pl.when(src == 1)
    def _():
        cross_copy.wait_send()
        on.wait_send()


def on_device(
    resid, token_ids, enc_weight, enc_bias, threshold, dec_self, dec_cross
):
    vmem = pl.BlockSpec(memory_space=pltpu.VMEM)
    hbm = pl.BlockSpec(memory_space=pl.ANY)
    dma = pltpu.SemaphoreType.DMA
    scratch = [
        pltpu.VMEM((NZ, NX, NY, 16, QUARTER), BF16),
        pltpu.VMEM((PLANE, D), BF16),
        pltpu.VMEM((2, D, LAT), BF16),
        pltpu.VMEM((2, LAT, D), BF16),
        pltpu.VMEM((2, LAT, D), BF16),
        pltpu.VMEM((2, 1, LAT), F32),
        pltpu.VMEM((2, 1, LAT), F32),
        pltpu.VMEM((2, PLANE, 2 * LAT), BF16),
        pltpu.VMEM((2, PLANE, 2 * LAT), BF16),
        pltpu.VMEM((PLANE, 2 * PLANE), BF16),
        pltpu.VMEM((PLANE, 2 * LAT), BF16),
        pltpu.VMEM((PLANE, 2 * LAT), BF16),
        pltpu.VMEM((TILES, NX, NY, NZ * ROWS, TILE), F32),
        pltpu.VMEM((TILES, NX, NY, NZ * ROWS, TILE), BF16),
        pltpu.VMEM((TILES, NY, NZ * ROWS, TILE), F32),
        pltpu.VMEM((TILES, NY, NZ * ROWS, TILE), BF16),
        pltpu.VMEM((NZ, TILES, 16, TILE // 4), BF16),
        pltpu.VMEM((NZ, TILES, 16, TILE // 4), F32),
        pltpu.VMEM((TILES, NY, NZ * ROWS, TILE), BF16),
        pltpu.VMEM((TILES, NY, NZ * ROWS, TILE), BF16),
        pltpu.VMEM((TILES, NY, NX, NZ * ROWS, TILE), BF16),
        pltpu.VMEM((TILES, NZ * ROWS, TILE), BF16),
        pltpu.VMEM((NZ, TILES, 16, TILE // 4), BF16),
        dma((3,)),
        dma((5,)),
        dma((5,)),
        dma((3,)),
        dma((3,)),
        dma((NZ,)),
        dma((NZ,)),
        dma((NZ, NY)),
        dma((NZ, NY)),
        dma((NZ,)),
        dma((NZ,)),
        dma((NZ,)),
        dma((NZ,)),
        dma((NZ, NY)),
        dma((NZ, NY)),
        dma((TILES, NY)),
        dma((TILES, NY)),
        dma((TILES, NY)),
        dma((TILES, NY)),
        dma((len(Z_GROUPS), NZ)),
        dma((len(Z_GROUPS), NZ)),
    ]
    return pl.pallas_call(
        kernel,
        out_shape=jax.ShapeDtypeStruct((1, ROWS, D), BF16),
        in_specs=[vmem, vmem, vmem, vmem, hbm, hbm, hbm],
        out_specs=vmem,
        scratch_shapes=scratch,
        compiler_params=pltpu.CompilerParams(
            collective_id=0, has_side_effects=True, vmem_limit_bytes=58 * 2**20
        ),
    )(
        token_ids.reshape(1, 2 * PLANE),
        resid,
        enc_bias,
        threshold,
        enc_weight,
        dec_self,
        dec_cross,
    )


def solution(mesh):
    in_specs = (
        P("src", "lat", None),
        P(),
        P("src", None, "lat"),
        P("src", "lat"),
        P("src", "lat"),
        P("src", "lat", None),
        P("lat", None),
    )
    out_specs = P("src", "lat", None)
    return jax.shard_map(
        on_device, mesh=mesh, in_specs=in_specs, out_specs=out_specs, check_vma=False
    )
```

```python
import jax
import jax.numpy as jnp
from jax import lax
from jax.experimental import pallas as pl
from jax.experimental.pallas import tpu as pltpu
from jax.sharding import PartitionSpec as P

MESH = pl.DeviceIdType.MESH
BF16, F32 = jnp.bfloat16, jnp.float32

NZ, NX, NY = 8, 2, 4
ROWS = 4
D, LAT = 4096, 256
PLANE = NZ * NX * NY * ROWS
QUARTER = D // 4
ZLAST = 256
XFIRST = {0: 384, 1: 256, 2: 384, 3: 256, 4: 384, 5: 256, 6: 384, 7: 256}
TILE = 512
TILES = D // TILE
Z_TILES = 2
Y_TILES = (2, 5)
GROUPS = ((0, 1), (1, 2), (2, 4), (4, 6), (6, 8))
Z_ORDER = (0, 1, 7, 2, 6, 3, 5, 4)
Y_ORDER = (1, 3, 2)
PLANE_ORDER = ((0, 1), (0, 3), (1, 0), (0, 2), (1, 1), (1, 3), (1, 2))


def kernel(
    ids_hbm,
    resid,
    bias,
    thresh,
    enc_hbm,
    own_hbm,
    cross_hbm,
    out,
    blocks,
    rows,
    enc,
    own_dec,
    cross_dec,
    bias2,
    thresh2,
    codes,
    earlier,
    select,
    mixed,
    mixed_cross,
    part,
    send1,
    half,
    send2,
    send3,
    last,
    got_x1,
    got_y2,
    got_y1,
    got_x2,
    got_z,
    got_a,
    got_h,
    row_buf,
    ids_buf,
    local_sem,
    sent,
    core_recv,
    code_recv,
    z_recv,
    cy_recv,
    cx_recv,
    bx_recv,
    by_recv,
    a1_recv,
    az_recv,
    r1_recv,
    r2_recv,
    s1_recv,
    s2_recv,
    s3_recv,
):
    src = lax.axis_index("src")
    lat = lax.axis_index("lat")
    core = lax.rem(lat, 2)
    y = lax.rem(lat // 2, NY)
    x = lax.rem(lat // (2 * NY), NX)
    z = lat // (2 * NY * NX)

    def at(z, x, y, core):
        return (src, ((z * NX + x) * NY + y) * 2 + core)

    def zp(dz):
        return lax.rem(z + NZ - dz, NZ)

    def zn(dz):
        return lax.rem(z + dz, NZ)

    def xn(dx):
        return lax.rem(x + dx, NX)

    def yn(dy):
        return lax.rem(y + dy, NY)

    other_core = at(z, x, y, 1 - core)
    other_src = (1 - src, lat)
    other_x = at(z, 1 - x, y, core)

    def remote(src_ref, dst_ref, recv, device):
        return pltpu.make_async_remote_copy(
            src_ref=src_ref,
            dst_ref=dst_ref,
            send_sem=sent,
            recv_sem=recv,
            device_id=device,
            device_id_type=MESH,
        )

    def arrived(ref, recv):
        remote(ref, ref, recv, other_core).wait_recv()

    started = []

    def go(make, *args):
        make(*args).start()
        started.append((make, args))

    locals_ = [
        pltpu.make_async_copy(enc_hbm.at[0], enc.at[core], local_sem.at[0]),
        pltpu.make_async_copy(own_hbm.at[0], own_dec.at[core], local_sem.at[1]),
        pltpu.make_async_copy(cross_hbm, cross_dec.at[core], local_sem.at[2]),
        pltpu.make_async_copy(resid.at[0], row_buf, local_sem.at[3]),
        pltpu.make_async_copy(ids_hbm, ids_buf, local_sem.at[4]),
        pltpu.make_async_copy(bias, bias2.at[core], local_sem.at[5]),
        pltpu.make_async_copy(thresh, thresh2.at[core], local_sem.at[6]),
    ]
    for n in (3, 4, 5, 6, 0, 1, 2):
        locals_[n].start()

    barrier = pltpu.get_barrier_semaphore()
    peers = [at(zn(o), x, y, core) for o in range(1, NZ)]
    peers += [at(z, xn(dx), yn(dy), core) for dx, dy in PLANE_ORDER]
    peers += [other_core, other_src]
    for peer in peers:
        pl.semaphore_signal(barrier, inc=1, device_id=peer, device_id_type=MESH)

    locals_[3].wait()
    mine = row_buf[...].astype(F32)
    blocks[z, x, y] = jnp.concatenate(
        [mine[:, q * QUARTER : (q + 1) * QUARTER] for q in range(4)], axis=0
    ).astype(BF16)

    pl.semaphore_wait(barrier, len(peers))

    a_cols, z_cols = pl.ds(0, ZLAST), pl.ds(ZLAST, QUARTER - ZLAST)

    def b_cols(dz):
        return pl.ds(ZLAST, XFIRST[dz])

    def c_cols(dz):
        return pl.ds(ZLAST + XFIRST[dz], QUARTER - ZLAST - XFIRST[dz])

    def same(ref, recv, device):
        return remote(ref, ref, recv, device)

    def z_copy(o):
        ref = blocks.at[z, x, y, :, z_cols]
        return same(ref, z_recv.at[o], at(zn(o), x, y, core))

    def a1_copy(dx, dy):
        ref = blocks.at[z, x, y, :, a_cols]
        peer = at(z, xn(dx), yn(dy), core)
        return same(ref, a1_recv.at[0], peer)

    def az_copy(n):
        dz, o = ((0, 1), (0, 7), (0, 2), (0, 6), (2, 1), (6, 7), (2, 2), (6, 6))[n]
        xs = slice(None) if n < 6 else n - 6
        ref = blocks.at[zp(dz), xs, :, :, a_cols]
        return same(ref, az_recv.at[n], at(zn(o), x, y, core))

    AZ_OF = {1: (0,), 7: (1,), 2: (2,), 6: (3,), 3: (4,), 5: (5,), 4: (6, 7)}

    def cy_copy(dz, o):
        ref = blocks.at[zp(dz), x, y, :, c_cols(dz)]
        return same(ref, cy_recv.at[dz], at(z, x, yn(o), core))

    def bx_copy(dz):
        ref = blocks.at[zp(dz), x, y, :, b_cols(dz)]
        return same(ref, bx_recv.at[dz], other_x)

    def cx_copy(dz):
        ref = blocks.at[zp(dz), x, :, :, c_cols(dz)]
        return same(ref, cx_recv.at[dz], other_x)

    def by_copy(dz, o):
        ref = blocks.at[zp(dz), :, y, :, b_cols(dz)]
        return same(ref, by_recv.at[dz], at(z, x, yn(o), core))

    def second(dz):
        if dz:
            z_copy(dz).wait_recv()
        for o in Y_ORDER:
            go(cy_copy, dz, o)
        go(bx_copy, dz)

    def third(dz):
        bx_copy(dz).wait_recv()
        for o in Y_ORDER:
            go(by_copy, dz, o)
        arrived(blocks.at[zp(dz), x, pl.ds(0, 3), :, c_cols(dz)], cy_recv.at[dz])
        go(cx_copy, dz)

    def plane_done():
        arrived(blocks.at[pl.ds(0, 7), x, y, :, a_cols], a1_recv.at[0])
        for n in range(4):
            go(az_copy, n)

    def pass_on():
        for dz in (2, 6):
            for n in AZ_OF[dz]:
                az_copy(n).wait_recv()
            go(az_copy, 4 if dz == 2 else 5)
            go(az_copy, 6 if dz == 2 else 7)

    for o in Z_ORDER[1:]:
        go(z_copy, o)
    for dx, dy in PLANE_ORDER:
        go(a1_copy, dx, dy)
    second(0)

    def core_copy(n):
        src_ref, dst_ref = (
            (bias, bias2.at[core]),
            (thresh, thresh2.at[core]),
            (enc_hbm.at[0], enc.at[core]),
            (own_hbm.at[0], own_dec.at[core]),
            (cross_hbm, cross_dec.at[core]),
        )[n]
        return remote(src_ref, dst_ref, core_recv.at[n], other_core)

    for n in range(4):
        go(core_copy, n)

    @pl.when(src == 1)
    def _():
        core_copy(4).start()

    locals_[4].wait()
    shape = (2 * PLANE, 2 * PLANE)
    j = lax.broadcasted_iota(jnp.int32, shape, 0)
    plane, within = j // PLANE, j % PLANE
    pool = (within // ROWS) * (2 * ROWS) + plane * ROWS + within % ROWS
    named = (jnp.broadcast_to(ids_buf[...], shape) == pool).astype(F32).astype(BF16)
    i = lax.broadcasted_iota(jnp.int32, shape, 0)
    t = lax.broadcasted_iota(jnp.int32, shape, 1)
    ir, iz, ixy = i % ROWS, (i // ROWS) % NZ, (i // (ROWS * NZ)) % (NX * NY)
    token = jnp.where(
        i < PLANE,
        (iz * NX * NY + ixy) * (2 * ROWS) + core * ROWS + ir,
        ((i - PLANE) // ROWS) * (2 * ROWS) + core * ROWS + ir,
    )
    order = (t == token).astype(F32).astype(BF16)
    select[...] = lax.dot_general(
        order, named, (((1,), (1,)), ((), ())), preferred_element_type=F32
    ).astype(BF16)

    second(1)
    second(7)
    plane_done()
    second(2)
    third(0)
    second(6)
    third(1)
    second(3)
    third(7)
    second(5)
    third(2)
    second(4)
    pass_on()
    third(6)
    third(3)
    third(5)
    third(4)

    def unpack(dz):
        zz = zp(dz)
        for xx in range(NX):
            four = [blocks[zz, xx, yy].astype(F32) for yy in range(NY)]
            start = pl.multiple_of((zz * NX + xx) * (NY * ROWS), NY * ROWS)
            for q in range(4):
                rows[pl.ds(start, NY * ROWS), q * QUARTER : (q + 1) * QUARTER] = (
                    jnp.concatenate([b[4 * q : 4 * q + 4] for b in four], axis=0)
                ).astype(BF16)

    for dz in Z_ORDER:
        for n in AZ_OF.get(dz, ()):
            if n not in AZ_OF[2] + AZ_OF[6]:
                az_copy(n).wait_recv()
        arrived(blocks.at[zp(dz), :, pl.ds(0, 3), :, b_cols(dz)], by_recv.at[dz])
        cx_copy(dz).wait_recv()
        unpack(dz)

    def code_copy(h):
        ref = codes.at[h, core]
        return same(ref, code_recv.at[0, h], other_core)

    def over_copy(h):
        return remote(
            codes.at[h, core],
            earlier.at[h, core],
            code_recv.at[1, h],
            other_src,
        )

    def on_copy(h):
        ref = earlier.at[h, core]
        return same(ref, code_recv.at[2, h], other_core)

    for n in (0, 5, 6):
        locals_[n].wait()
    for n in range(3):
        core_copy(n).wait_recv()
    for h in range(2):
        pre = jnp.dot(rows[...], enc[h], preferred_element_type=F32) + bias2[h]
        gate = jnp.clip((pre - thresh2[h]) / 0.1, 0.0, 1.0)
        codes[h, core] = (pre * gate).astype(BF16)

        @pl.when(src == 0)
        def _():
            over_copy(h).start()

        go(code_copy, h)

    def permute(ref, into, h):
        into[:, h * LAT : (h + 1) * LAT] = jnp.dot(
            select[...], ref[h].reshape(2 * PLANE, LAT), preferred_element_type=F32
        ).astype(BF16)

    for h in range(2):
        code_copy(h).wait_recv()
        permute(codes, mixed, h)
    locals_[1].wait()
    core_copy(3).wait_recv()
    locals_[2].wait()

    def product(left, right, n):
        start = PLANE if n < Z_TILES else 0
        return sum(
            jnp.dot(
                left[start : start + PLANE, h * LAT : (h + 1) * LAT],
                right[h, :, n * TILE : (n + 1) * TILE],
                preferred_element_type=F32,
            )
            for h in range(2)
        ).reshape(NX, NY, NZ * ROWS, TILE)

    def y1_copy(n, o):
        return remote(
            send1.at[n, :, yn(o)],
            got_y1.at[n, o],
            s1_recv.at[n],
            at(z, x, yn(o), core),
        )

    def x1_copy(n):
        return remote(
            send1.at[n, 1 - x], got_x1.at[n], s1_recv.at[n], other_x
        )

    def y2_copy(n, o):
        return remote(
            send2.at[n, yn(o)],
            got_y2.at[n, o],
            s2_recv.at[n],
            at(z, x, yn(o), core),
        )

    def x2_copy(n):
        return remote(
            send2.at[n, 1 - x], got_x2.at[n], s2_recv.at[n], other_x
        )

    def r1_copy(n, k):
        o, to, first, count = (
            (1, 1, 0, 32),
            (7, 7, 0, 32),
            (3, 1, 0, 32),
            (5, 7, 0, 32),
            (4, 2, 0, 16),
            (4, 6, 16, 16),
        )[k]
        zz = zn(o)
        return remote(
            send1.at[n, zz // NY, zz % NY, pl.ds(first, count)],
            got_a.at[n, k] if k < 4 else got_h.at[n, k - 4],
            r1_recv.at[n, k],
            at(zn(to), x, y, core),
        )

    def r2_copy(n, k):
        return remote(
            send2.at[n, k],
            got_a.at[n, 4 + k],
            r2_recv.at[n, k],
            at(zn((2, 6)[k]), x, y, core),
        )

    def last_copy(g, k):
        first, end = GROUPS[g]
        tiles = pl.ds(first, end - first)
        if first < Z_TILES:
            xx, yy = xn(k // NY), yn(k % NY)
            peer, place = at(z, xx, yy, core), xx * NY + yy
        else:
            peer, place = at(zn(k), x, y, core), zn(k)
        return remote(
            send3.at[place, tiles],
            got_z.at[k, tiles],
            s3_recv.at[g],
            peer,
        )

    def first_copies(n):
        if n < Z_TILES:
            return [(r1_copy, (n, k)) for k in (4, 5, 2, 3, 0, 1)]
        if n in Y_TILES:
            return [(y1_copy, (n, o)) for o in Y_ORDER]
        return [(x1_copy, (n,))]

    def stage1(n, total):
        send1[n] = total.astype(BF16)
        for make, args in first_copies(n):
            make(*args).start()

    def stage2(n):
        if n < Z_TILES:
            for k in (2, 3, 4, 5):
                r1_copy(n, k).wait_recv()
            for k in range(2):
                zz = zn((2, 6)[k])
                total = part[n, zz // NY, zz % NY] + got_a[n, 2 + k].astype(F32)
                more = got_h[n, k].astype(F32)
                top, low = total[:16], total[16:]
                if k == 0:
                    top += more
                else:
                    low += more
                send2[n, k, 0:16] = top.astype(BF16)
                send2[n, k, 16:32] = low.astype(BF16)
                go(r2_copy, n, k)
        elif n in Y_TILES:
            total = part[n, :, y]
            arrived(got_y1.at[n, pl.ds(1, 3)], s1_recv.at[n])
            for o in Y_ORDER:
                total += got_y1[n, o].astype(F32)
            half[n, 0:NX] = total
            send2[n, 0:NX] = total.astype(BF16)
            go(x2_copy, n)
        else:
            x1_copy(n).wait_recv()
            total = part[n, x] + got_x1[n].astype(F32)
            half[n] = total
            send2[n] = total.astype(BF16)
            for o in Y_ORDER:
                go(y2_copy, n, o)

    def stage3(n):
        if n < Z_TILES:
            total = part[n, z // NY, z % NY]
            for k in range(2):
                r1_copy(n, k).wait_recv()
                total += got_a[n, k].astype(F32)
            for k in range(2):
                r2_copy(n, k).wait_recv()
                total += got_a[n, 4 + k].astype(F32)
        elif n in Y_TILES:
            x2_copy(n).wait_recv()
            total = half[n, x] + got_x2[n].astype(F32)
        else:
            total = half[n, y]
            arrived(got_y2.at[n, pl.ds(1, 3)], s2_recv.at[n])
            for o in Y_ORDER:
                total += got_y2[n, o].astype(F32)
        step = TILE // 4
        for k in range(8):
            block = jnp.concatenate(
                [
                    total[k * ROWS : (k + 1) * ROWS, q * step : (q + 1) * step]
                    for q in range(4)
                ],
                axis=0,
            )
            last[k, n] = block
            send3[k, n] = block.astype(BF16)
        for g, (_, end) in enumerate(GROUPS):
            if n == end - 1:
                for k in (4, 3, 5, 2, 6, 1, 7):
                    go(last_copy, g, k)

    def finish(g):
        first, end = GROUPS[g]
        arrived(got_z.at[pl.ds(1, 7), pl.ds(first, end - first)], s3_recv.at[g])
        step = TILE // 4
        for n in range(first, end):
            total = last[x * NY + y if n < Z_TILES else z, n]
            for k in range(1, 8):
                total += got_z[k, n].astype(F32)
            for q in range(4):
                out[0, :, n * TILE + q * step : n * TILE + (q + 1) * step] = total[
                    q * ROWS : (q + 1) * ROWS
                ].astype(BF16)

    for n in range(TILES):
        started.extend(first_copies(n))
        part[n] = product(mixed, own_dec, n)

        @pl.when(src == 0)
        def _():
            stage1(n, part[n])

    @pl.when(src == 1)
    def _():
        core_copy(4).wait_recv()
        for h in range(2):
            over_copy(h).wait_recv()
            on_copy(h).start()
        for h in range(2):
            on_copy(h).wait_recv()
            permute(earlier, mixed_cross, h)
        for n in range(TILES):
            total = part[n] + product(mixed_cross, cross_dec, n)
            part[n] = total
            stage1(n, total)

    for n in range(TILES + 2):
        if n < TILES:
            stage2(n)
        if n >= 2:
            stage3(n - 2)
    for g in range(len(GROUPS)):
        finish(g)

    for make, args in started:
        make(*args).wait_send()

    @pl.when(src == 0)
    def _():
        for h in range(2):
            over_copy(h).wait_send()

    @pl.when(src == 1)
    def _():
        core_copy(4).wait_send()
        for h in range(2):
            on_copy(h).wait_send()


def on_device(
    resid, token_ids, enc_weight, enc_bias, threshold, dec_self, dec_cross
):
    vmem = pl.BlockSpec(memory_space=pltpu.VMEM)
    hbm = pl.BlockSpec(memory_space=pl.ANY)
    dma = pltpu.SemaphoreType.DMA
    scratch = [
        pltpu.VMEM((NZ, NX, NY, 16, QUARTER), BF16),
        pltpu.VMEM((PLANE, D), BF16),
        pltpu.VMEM((2, D, LAT), BF16),
        pltpu.VMEM((2, LAT, D), BF16),
        pltpu.VMEM((2, LAT, D), BF16),
        pltpu.VMEM((2, 1, LAT), F32),
        pltpu.VMEM((2, 1, LAT), F32),
        pltpu.VMEM((2, 2, PLANE, LAT), BF16),
        pltpu.VMEM((2, 2, PLANE, LAT), BF16),
        pltpu.VMEM((2 * PLANE, 2 * PLANE), BF16),
        pltpu.VMEM((2 * PLANE, 2 * LAT), BF16),
        pltpu.VMEM((2 * PLANE, 2 * LAT), BF16),
        pltpu.VMEM((TILES, NX, NY, NZ * ROWS, TILE), F32),
        pltpu.VMEM((TILES, NX, NY, NZ * ROWS, TILE), BF16),
        pltpu.VMEM((TILES, NY, NZ * ROWS, TILE), F32),
        pltpu.VMEM((TILES, NY, NZ * ROWS, TILE), BF16),
        pltpu.VMEM((NZ, TILES, 16, TILE // 4), BF16),
        pltpu.VMEM((NZ, TILES, 16, TILE // 4), F32),
        pltpu.VMEM((TILES, NY, NZ * ROWS, TILE), BF16),
        pltpu.VMEM((TILES, NY, NZ * ROWS, TILE), BF16),
        pltpu.VMEM((TILES, NY, NX, NZ * ROWS, TILE), BF16),
        pltpu.VMEM((TILES, NZ * ROWS, TILE), BF16),
        pltpu.VMEM((NZ, TILES, 16, TILE // 4), BF16),
        pltpu.VMEM((Z_TILES, 6, NZ * ROWS, TILE), BF16),
        pltpu.VMEM((Z_TILES, 2, 16, TILE), BF16),
        pltpu.VMEM((ROWS, D), BF16),
        pltpu.VMEM((1, 2 * PLANE), jnp.int32),
        dma((7,)),
        dma,
        dma((5,)),
        dma((3, 2)),
        dma((NZ,)),
        dma((NZ,)),
        dma((NZ,)),
        dma((NZ,)),
        dma((NZ,)),
        dma((1,)),
        dma((8,)),
        dma((Z_TILES, 6)),
        dma((Z_TILES, 2)),
        dma((TILES,)),
        dma((TILES,)),
        dma((len(GROUPS),)),
    ]
    return pl.pallas_call(
        kernel,
        out_shape=jax.ShapeDtypeStruct((1, ROWS, D), BF16),
        in_specs=[hbm] * 7,
        out_specs=vmem,
        scratch_shapes=scratch,
        compiler_params=pltpu.CompilerParams(
            collective_id=0, has_side_effects=True, vmem_limit_bytes=58 * 2**20
        ),
    )(
        token_ids.reshape(1, 2 * PLANE),
        resid,
        enc_bias,
        threshold,
        enc_weight,
        dec_self,
        dec_cross,
    )


def solution(mesh):
    in_specs = (
        P("src", "lat", None),
        P(),
        P("src", None, "lat"),
        P("src", "lat"),
        P("src", "lat"),
        P("src", "lat", None),
        P("lat", None),
    )
    out_specs = P("src", "lat", None)
    return jax.shard_map(
        on_device, mesh=mesh, in_specs=in_specs, out_specs=out_specs, check_vma=False
    )
```

```python
import jax
import jax.numpy as jnp
from jax import lax
from jax.experimental import pallas as pl
from jax.experimental.pallas import tpu as pltpu
from jax.sharding import PartitionSpec as P

MESH = pl.DeviceIdType.MESH
BF16, F32 = jnp.bfloat16, jnp.float32

NZ, NX, NY = 8, 2, 4
ROWS = 4
D, LAT = 4096, 256
PLANE = NZ * NX * NY * ROWS
QUARTER = D // 4
ZLAST = 256
XFIRST = {i: 384 for i in range(8)}
TILE = 512
TILES = D // TILE
Z_TILES = 2
Y_TILES = (2, 4, 6)
GROUPS = ((0, 1), (1, 2), (2, 4), (4, 6), (6, 8))
Z_ORDER = (0, 1, 7, 2, 6, 3, 5, 4)
Y_ORDER = (1, 3, 2)
TILE_ORDER = (2, 3, 0, 4, 5, 1, 6, 7)
LAG = 4
PARTS = ((0, 5), (5, 8))
PLANE_ORDER = ((0, 1), (0, 3), (1, 0), (0, 2), (1, 1), (1, 3), (1, 2))


def kernel(
    ids_hbm,
    resid,
    bias,
    thresh,
    enc_hbm,
    own_hbm,
    cross_hbm,
    out,
    blocks,
    rows,
    enc,
    own_dec,
    cross_dec,
    bias2,
    thresh2,
    codes,
    earlier,
    select,
    mixed,
    mixed_cross,
    part,
    send1,
    half,
    send2,
    send3,
    last,
    got_x1,
    got_y2,
    got_y1,
    got_x2,
    got_z,
    got_a,
    got_h,
    row_buf,
    ids_buf,
    local_sem,
    sent,
    core_recv,
    code_recv,
    z_recv,
    cy_recv,
    cx_recv,
    bx_recv,
    by_recv,
    a1_recv,
    az_recv,
    r1_recv,
    r2_recv,
    s1_recv,
    s2_recv,
    s3_recv,
):
    src = lax.axis_index("src")
    lat = lax.axis_index("lat")
    core = lax.rem(lat, 2)
    y = lax.rem(lat // 2, NY)
    x = lax.rem(lat // (2 * NY), NX)
    z = lat // (2 * NY * NX)

    def at(z, x, y, core):
        return (src, ((z * NX + x) * NY + y) * 2 + core)

    def zp(dz):
        return lax.rem(z + NZ - dz, NZ)

    def zn(dz):
        return lax.rem(z + dz, NZ)

    def xn(dx):
        return lax.rem(x + dx, NX)

    def yn(dy):
        return lax.rem(y + dy, NY)

    other_core = at(z, x, y, 1 - core)
    other_src = (1 - src, lat)
    other_x = at(z, 1 - x, y, core)

    def remote(src_ref, dst_ref, recv, device):
        return pltpu.make_async_remote_copy(
            src_ref=src_ref,
            dst_ref=dst_ref,
            send_sem=sent,
            recv_sem=recv,
            device_id=device,
            device_id_type=MESH,
        )

    def arrived(ref, recv):
        remote(ref, ref, recv, other_core).wait_recv()

    started = []

    def go(make, *args):
        make(*args).start()
        started.append((make, args))

    locals_ = [
        pltpu.make_async_copy(enc_hbm.at[0], enc.at[core], local_sem.at[0]),
        pltpu.make_async_copy(own_hbm.at[0], own_dec.at[core], local_sem.at[1]),
        pltpu.make_async_copy(cross_hbm, cross_dec.at[core], local_sem.at[2]),
        pltpu.make_async_copy(resid.at[0], row_buf, local_sem.at[3]),
        pltpu.make_async_copy(ids_hbm, ids_buf, local_sem.at[4]),
        pltpu.make_async_copy(bias, bias2.at[core], local_sem.at[5]),
        pltpu.make_async_copy(thresh, thresh2.at[core], local_sem.at[6]),
    ]
    for n in (3, 4, 5, 6, 0, 1, 2):
        locals_[n].start()

    barrier = pltpu.get_barrier_semaphore()
    peers = [at(zn(o), x, y, core) for o in range(1, NZ)]
    peers += [at(z, xn(dx), yn(dy), core) for dx, dy in PLANE_ORDER]
    peers += [other_core, other_src]
    for peer in peers:
        pl.semaphore_signal(barrier, inc=1, device_id=peer, device_id_type=MESH)

    locals_[3].wait()
    mine = row_buf[...].astype(F32)
    blocks[z, x, y] = jnp.concatenate(
        [mine[:, q * QUARTER : (q + 1) * QUARTER] for q in range(4)], axis=0
    ).astype(BF16)

    pl.semaphore_wait(barrier, len(peers))

    a_cols, z_cols = pl.ds(0, ZLAST), pl.ds(ZLAST, QUARTER - ZLAST)

    def b_cols(dz):
        return pl.ds(ZLAST, XFIRST[dz])

    def c_cols(dz):
        return pl.ds(ZLAST + XFIRST[dz], QUARTER - ZLAST - XFIRST[dz])

    def same(ref, recv, device):
        return remote(ref, ref, recv, device)

    def z_copy(o):
        ref = blocks.at[z, x, y, :, z_cols]
        return same(ref, z_recv.at[o], at(zn(o), x, y, core))

    def a1_copy(dx, dy):
        ref = blocks.at[z, x, y, :, a_cols]
        peer = at(z, xn(dx), yn(dy), core)
        return same(ref, a1_recv.at[0], peer)

    def az_copy(n):
        dz, o = ((0, 1), (0, 7), (0, 2), (0, 6), (2, 1), (6, 7), (2, 2), (6, 6))[n]
        xs = slice(None) if n < 6 else n - 6
        ref = blocks.at[zp(dz), xs, :, :, a_cols]
        return same(ref, az_recv.at[n], at(zn(o), x, y, core))

    AZ_OF = {1: (0,), 7: (1,), 2: (2,), 6: (3,), 3: (4,), 5: (5,), 4: (6, 7)}

    def cy_copy(dz, o):
        ref = blocks.at[zp(dz), x, y, :, c_cols(dz)]
        return same(ref, cy_recv.at[dz], at(z, x, yn(o), core))

    def bx_copy(dz):
        ref = blocks.at[zp(dz), x, y, :, b_cols(dz)]
        return same(ref, bx_recv.at[dz], other_x)

    def cx_copy(dz):
        ref = blocks.at[zp(dz), x, :, :, c_cols(dz)]
        return same(ref, cx_recv.at[dz], other_x)

    def by_copy(dz, o):
        ref = blocks.at[zp(dz), :, y, :, b_cols(dz)]
        return same(ref, by_recv.at[dz], at(z, x, yn(o), core))

    def second(dz):
        if dz:
            z_copy(dz).wait_recv()
        for o in Y_ORDER:
            go(cy_copy, dz, o)
        go(bx_copy, dz)

    def third(dz):
        bx_copy(dz).wait_recv()
        for o in Y_ORDER:
            go(by_copy, dz, o)
        arrived(blocks.at[zp(dz), x, pl.ds(0, 3), :, c_cols(dz)], cy_recv.at[dz])
        go(cx_copy, dz)

    def plane_done():
        arrived(blocks.at[pl.ds(0, 7), x, y, :, a_cols], a1_recv.at[0])
        for n in range(4):
            go(az_copy, n)

    def pass_on():
        for dz in (2, 6):
            for n in AZ_OF[dz]:
                az_copy(n).wait_recv()
            go(az_copy, 4 if dz == 2 else 5)
            go(az_copy, 6 if dz == 2 else 7)

    for o in Z_ORDER[1:]:
        go(z_copy, o)
    for dx, dy in PLANE_ORDER:
        go(a1_copy, dx, dy)
    second(0)

    def core_copy(n):
        src_ref, dst_ref = (
            (bias, bias2.at[core]),
            (thresh, thresh2.at[core]),
            (enc_hbm.at[0], enc.at[core]),
            (own_hbm.at[0], own_dec.at[core]),
            (cross_hbm, cross_dec.at[core]),
        )[n]
        return remote(src_ref, dst_ref, core_recv.at[n], other_core)

    for n in range(4):
        go(core_copy, n)

    @pl.when(src == 1)
    def _():
        core_copy(4).start()

    locals_[4].wait()
    shape = (2 * PLANE, 2 * PLANE)
    j = lax.broadcasted_iota(jnp.int32, shape, 0)
    plane, within = j // PLANE, j % PLANE
    step = within // (NX * NY * ROWS)
    far = jnp.where(step % 2 == 0, step // 2, NZ - (step + 1) // 2)
    pool = (z + far) % NZ * (NX * NY) + (within // ROWS) % (NX * NY)
    pool = pool * (2 * ROWS) + plane * ROWS + within % ROWS
    named = (jnp.broadcast_to(ids_buf[...], shape) == pool).astype(F32).astype(BF16)
    i = lax.broadcasted_iota(jnp.int32, shape, 0)
    t = lax.broadcasted_iota(jnp.int32, shape, 1)
    ir, iz, ixy = i % ROWS, (i // ROWS) % NZ, (i // (ROWS * NZ)) % (NX * NY)
    token = jnp.where(
        i < PLANE,
        (iz * NX * NY + ixy) * (2 * ROWS) + core * ROWS + ir,
        ((i - PLANE) // ROWS) * (2 * ROWS) + core * ROWS + ir,
    )
    order = (t == token).astype(F32).astype(BF16)
    select[...] = lax.dot_general(
        order, named, (((1,), (1,)), ((), ())), preferred_element_type=F32
    ).astype(BF16)

    second(1)
    second(7)
    plane_done()
    second(2)
    second(6)
    third(0)
    second(3)
    second(5)
    third(1)
    third(7)
    second(4)
    pass_on()
    third(2)
    third(6)
    third(3)
    third(5)
    third(4)

    def unpack(place, dz):
        zz = zp(dz)
        for xx in range(NX):
            four = [blocks[zz, xx, yy].astype(F32) for yy in range(NY)]
            start = (place * NX + xx) * (NY * ROWS)
            for q in range(4):
                rows[start : start + NY * ROWS, q * QUARTER : (q + 1) * QUARTER] = (
                    jnp.concatenate([b[4 * q : 4 * q + 4] for b in four], axis=0)
                ).astype(BF16)

    def bounds(c):
        first, end = PARTS[c]
        return first * NX * NY * ROWS, (end - first) * NX * NY * ROWS

    def code_copy(c):
        ref = codes.at[:, core, pl.ds(*bounds(c))]
        return same(ref, code_recv.at[0, c], other_core)

    def over_copy(c):
        return remote(
            codes.at[:, core, pl.ds(*bounds(c))],
            earlier.at[:, core, pl.ds(*bounds(c))],
            code_recv.at[1, c],
            other_src,
        )

    def on_copy(c):
        ref = earlier.at[:, core, pl.ds(*bounds(c))]
        return same(ref, code_recv.at[2, c], other_core)

    for c, (first, end) in enumerate(PARTS):
        for place in range(first, end):
            dz = Z_ORDER[place]
            for n in AZ_OF.get(dz, ()):
                if n not in AZ_OF[2] + AZ_OF[6]:
                    az_copy(n).wait_recv()
            arrived(blocks.at[zp(dz), :, pl.ds(0, 3), :, b_cols(dz)], by_recv.at[dz])
            cx_copy(dz).wait_recv()
            unpack(place, dz)
        if c == 0:
            for n in (0, 5, 6):
                locals_[n].wait()
            for n in range(3):
                core_copy(n).wait_recv()
        start, count = bounds(c)
        for h in range(2):
            pre = jnp.dot(
                rows[start : start + count], enc[h], preferred_element_type=F32
            )
            pre += bias2[h]
            gate = jnp.clip((pre - thresh2[h]) / 0.1, 0.0, 1.0)
            codes[h, core, start : start + count] = (pre * gate).astype(BF16)

        @pl.when(src == 0)
        def _():
            over_copy(c).start()

        go(code_copy, c)

    def permute(ref, into, h):
        into[:, h * LAT : (h + 1) * LAT] = jnp.dot(
            select[...], ref[h].reshape(2 * PLANE, LAT), preferred_element_type=F32
        ).astype(BF16)

    for c in range(2):
        code_copy(c).wait_recv()
    for h in range(2):
        permute(codes, mixed, h)
    locals_[1].wait()
    core_copy(3).wait_recv()
    locals_[2].wait()

    def product(left, right, n):
        start = PLANE if n < Z_TILES else 0
        return sum(
            jnp.dot(
                left[start : start + PLANE, h * LAT : (h + 1) * LAT],
                right[h, :, n * TILE : (n + 1) * TILE],
                preferred_element_type=F32,
            )
            for h in range(2)
        ).reshape(NX, NY, NZ * ROWS, TILE)

    def y1_copy(n, o):
        return remote(
            send1.at[n, :, yn(o)],
            got_y1.at[n, o],
            s1_recv.at[n],
            at(z, x, yn(o), core),
        )

    def x1_copy(n):
        return remote(
            send1.at[n, 1 - x], got_x1.at[n], s1_recv.at[n], other_x
        )

    def y2_copy(n, o):
        return remote(
            send2.at[n, yn(o)],
            got_y2.at[n, o],
            s2_recv.at[n],
            at(z, x, yn(o), core),
        )

    def x2_copy(n):
        return remote(
            send2.at[n, 1 - x], got_x2.at[n], s2_recv.at[n], other_x
        )

    def r1_copy(n, k):
        o, to, first, count = (
            (1, 1, 0, 32),
            (7, 7, 0, 32),
            (3, 1, 0, 32),
            (5, 7, 0, 32),
            (4, 2, 0, 16),
            (4, 6, 16, 16),
        )[k]
        zz = zn(o)
        return remote(
            send1.at[n, zz // NY, zz % NY, pl.ds(first, count)],
            got_a.at[n, k] if k < 4 else got_h.at[n, k - 4],
            r1_recv.at[n, k],
            at(zn(to), x, y, core),
        )

    def r2_copy(n, k):
        return remote(
            send2.at[n, k],
            got_a.at[n, 4 + k],
            r2_recv.at[n, k],
            at(zn((2, 6)[k]), x, y, core),
        )

    def last_copy(g, k):
        first, end = GROUPS[g]
        tiles = pl.ds(first, end - first)
        if first < Z_TILES:
            xx, yy = xn(k // NY), yn(k % NY)
            peer, place = at(z, xx, yy, core), xx * NY + yy
        else:
            peer, place = at(zn(k), x, y, core), zn(k)
        return remote(
            send3.at[place, tiles],
            got_z.at[k, tiles],
            s3_recv.at[g],
            peer,
        )

    def first_copies(n):
        if n < Z_TILES:
            return [(r1_copy, (n, k)) for k in (4, 5, 2, 3, 0, 1)]
        if n in Y_TILES:
            return [(y1_copy, (n, o)) for o in Y_ORDER]
        return [(x1_copy, (n,))]

    def stage1(n, total):
        send1[n] = total.astype(BF16)
        for make, args in first_copies(n):
            make(*args).start()

    def stage2(n):
        if n < Z_TILES:
            for k in (2, 3, 4, 5):
                r1_copy(n, k).wait_recv()
            for k in range(2):
                zz = zn((2, 6)[k])
                total = part[n, zz // NY, zz % NY] + got_a[n, 2 + k].astype(F32)
                more = got_h[n, k].astype(F32)
                top, low = total[:16], total[16:]
                if k == 0:
                    top += more
                else:
                    low += more
                send2[n, k, 0:16] = top.astype(BF16)
                send2[n, k, 16:32] = low.astype(BF16)
                go(r2_copy, n, k)
        elif n in Y_TILES:
            total = part[n, :, y]
            arrived(got_y1.at[n, pl.ds(1, 3)], s1_recv.at[n])
            for o in Y_ORDER:
                total += got_y1[n, o].astype(F32)
            half[n, 0:NX] = total
            send2[n, 0:NX] = total.astype(BF16)
            go(x2_copy, n)
        else:
            x1_copy(n).wait_recv()
            total = part[n, x] + got_x1[n].astype(F32)
            half[n] = total
            send2[n] = total.astype(BF16)
            for o in Y_ORDER:
                go(y2_copy, n, o)

    def stage3(n):
        if n < Z_TILES:
            total = part[n, z // NY, z % NY]
            for k in range(2):
                r1_copy(n, k).wait_recv()
                total += got_a[n, k].astype(F32)
            for k in range(2):
                r2_copy(n, k).wait_recv()
                total += got_a[n, 4 + k].astype(F32)
        elif n in Y_TILES:
            x2_copy(n).wait_recv()
            total = half[n, x] + got_x2[n].astype(F32)
        else:
            total = half[n, y]
            arrived(got_y2.at[n, pl.ds(1, 3)], s2_recv.at[n])
            for o in Y_ORDER:
                total += got_y2[n, o].astype(F32)
        step = TILE // 4
        for k in range(8):
            block = jnp.concatenate(
                [
                    total[k * ROWS : (k + 1) * ROWS, q * step : (q + 1) * step]
                    for q in range(4)
                ],
                axis=0,
            )
            last[k, n] = block
            send3[k, n] = block.astype(BF16)
        for g, (_, end) in enumerate(GROUPS):
            if n == end - 1:
                for k in (4, 3, 5, 2, 6, 1, 7):
                    go(last_copy, g, k)

    def finish(g):
        first, end = GROUPS[g]
        arrived(got_z.at[pl.ds(1, 7), pl.ds(first, end - first)], s3_recv.at[g])
        step = TILE // 4
        for n in range(first, end):
            total = last[x * NY + y if n < Z_TILES else z, n]
            for k in range(1, 8):
                total += got_z[k, n].astype(F32)
            for q in range(4):
                out[0, :, n * TILE + q * step : n * TILE + (q + 1) * step] = total[
                    q * ROWS : (q + 1) * ROWS
                ].astype(BF16)

    for n in TILE_ORDER:
        started.extend(first_copies(n))
        part[n] = product(mixed, own_dec, n)

        @pl.when(src == 0)
        def _():
            stage1(n, part[n])

    @pl.when(src == 1)
    def _():
        core_copy(4).wait_recv()
        for c in range(2):
            over_copy(c).wait_recv()
            on_copy(c).start()
        for c in range(2):
            on_copy(c).wait_recv()
        for h in range(2):
            permute(earlier, mixed_cross, h)
        for n in TILE_ORDER:
            total = part[n] + product(mixed_cross, cross_dec, n)
            part[n] = total
            stage1(n, total)

    for n in range(TILES + LAG):
        if n < TILES:
            stage2(n)
        if n >= LAG:
            stage3(n - LAG)
    for g in range(len(GROUPS)):
        finish(g)

    for make, args in started:
        make(*args).wait_send()

    @pl.when(src == 0)
    def _():
        for h in range(2):
            over_copy(h).wait_send()

    @pl.when(src == 1)
    def _():
        core_copy(4).wait_send()
        for h in range(2):
            on_copy(h).wait_send()


def on_device(
    resid, token_ids, enc_weight, enc_bias, threshold, dec_self, dec_cross
):
    vmem = pl.BlockSpec(memory_space=pltpu.VMEM)
    hbm = pl.BlockSpec(memory_space=pl.ANY)
    dma = pltpu.SemaphoreType.DMA
    scratch = [
        pltpu.VMEM((NZ, NX, NY, 16, QUARTER), BF16),
        pltpu.VMEM((PLANE, D), BF16),
        pltpu.VMEM((2, D, LAT), BF16),
        pltpu.VMEM((2, LAT, D), BF16),
        pltpu.VMEM((2, LAT, D), BF16),
        pltpu.VMEM((2, 1, LAT), F32),
        pltpu.VMEM((2, 1, LAT), F32),
        pltpu.VMEM((2, 2, PLANE, LAT), BF16),
        pltpu.VMEM((2, 2, PLANE, LAT), BF16),
        pltpu.VMEM((2 * PLANE, 2 * PLANE), BF16),
        pltpu.VMEM((2 * PLANE, 2 * LAT), BF16),
        pltpu.VMEM((2 * PLANE, 2 * LAT), BF16),
        pltpu.VMEM((TILES, NX, NY, NZ * ROWS, TILE), F32),
        pltpu.VMEM((TILES, NX, NY, NZ * ROWS, TILE), BF16),
        pltpu.VMEM((TILES, NY, NZ * ROWS, TILE), F32),
        pltpu.VMEM((TILES, NY, NZ * ROWS, TILE), BF16),
        pltpu.VMEM((NZ, TILES, 16, TILE // 4), BF16),
        pltpu.VMEM((NZ, TILES, 16, TILE // 4), F32),
        pltpu.VMEM((TILES, NY, NZ * ROWS, TILE), BF16),
        pltpu.VMEM((TILES, NY, NZ * ROWS, TILE), BF16),
        pltpu.VMEM((TILES, NY, NX, NZ * ROWS, TILE), BF16),
        pltpu.VMEM((TILES, NZ * ROWS, TILE), BF16),
        pltpu.VMEM((NZ, TILES, 16, TILE // 4), BF16),
        pltpu.VMEM((Z_TILES, 6, NZ * ROWS, TILE), BF16),
        pltpu.VMEM((Z_TILES, 2, 16, TILE), BF16),
        pltpu.VMEM((ROWS, D), BF16),
        pltpu.VMEM((1, 2 * PLANE), jnp.int32),
        dma((7,)),
        dma,
        dma((5,)),
        dma((3, 2)),
        dma((NZ,)),
        dma((NZ,)),
        dma((NZ,)),
        dma((NZ,)),
        dma((NZ,)),
        dma((1,)),
        dma((8,)),
        dma((Z_TILES, 6)),
        dma((Z_TILES, 2)),
        dma((TILES,)),
        dma((TILES,)),
        dma((len(GROUPS),)),
    ]
    return pl.pallas_call(
        kernel,
        out_shape=jax.ShapeDtypeStruct((1, ROWS, D), BF16),
        in_specs=[hbm] * 7,
        out_specs=vmem,
        scratch_shapes=scratch,
        compiler_params=pltpu.CompilerParams(
            collective_id=0, has_side_effects=True, vmem_limit_bytes=58 * 2**20
        ),
    )(
        token_ids.reshape(1, 2 * PLANE),
        resid,
        enc_bias,
        threshold,
        enc_weight,
        dec_self,
        dec_cross,
    )


def solution(mesh):
    in_specs = (
        P("src", "lat", None),
        P(),
        P("src", None, "lat"),
        P("src", "lat"),
        P("src", "lat"),
        P("src", "lat", None),
        P("lat", None),
    )
    out_specs = P("src", "lat", None)
    return jax.shard_map(
        on_device, mesh=mesh, in_specs=in_specs, out_specs=out_specs, check_vma=False
    )
```

```python
import jax
import jax.numpy as jnp
from jax import lax
from jax.experimental import pallas as pl
from jax.experimental.pallas import tpu as pltpu
from jax.sharding import PartitionSpec as P

MESH = pl.DeviceIdType.MESH
BF16, F32 = jnp.bfloat16, jnp.float32

NZ, NX, NY = 8, 2, 4
ROWS = 4
D, LAT = 4096, 256
PLANE = NZ * NX * NY * ROWS
QUARTER = D // 4
ZLAST = 256
XFIRST = {i: 384 for i in range(8)}
TILE = 512
TILES = D // TILE
Z_TILES = 2
Y_TILES = (2, 4, 6)
GROUPS = ((0, 1), (1, 2), (2, 4), (4, 6), (6, 8))
Z_ORDER = (0, 1, 7, 2, 6, 3, 5, 4)
Y_ORDER = (1, 3, 2)
TILE_ORDER = (2, 3, 0, 4, 5, 1, 6, 7)
LAG = 4
PARTS = ((0, 4), (4, 7), (7, 8))
PLANE_ORDER = ((0, 1), (0, 3), (1, 0), (0, 2), (1, 1), (1, 3), (1, 2))


def kernel(
    ids_hbm,
    resid,
    bias,
    thresh,
    enc_hbm,
    own_hbm,
    cross_hbm,
    out,
    blocks,
    rows,
    enc,
    own_dec,
    cross_dec,
    bias2,
    thresh2,
    codes,
    earlier,
    select,
    mixed,
    mixed_cross,
    part,
    send1,
    half,
    send2,
    send3,
    last,
    got_x1,
    got_y2,
    got_y1,
    got_x2,
    got_z,
    got_a,
    got_h,
    row_buf,
    ids_buf,
    local_sem,
    sent,
    core_recv,
    code_recv,
    z_recv,
    cy_recv,
    cx_recv,
    bx_recv,
    by_recv,
    a1_recv,
    az_recv,
    r1_recv,
    r2_recv,
    s1_recv,
    s2_recv,
    s3_recv,
):
    src = lax.axis_index("src")
    lat = lax.axis_index("lat")
    core = lax.rem(lat, 2)
    y = lax.rem(lat // 2, NY)
    x = lax.rem(lat // (2 * NY), NX)
    z = lat // (2 * NY * NX)

    def at(z, x, y, core):
        return (src, ((z * NX + x) * NY + y) * 2 + core)

    def zp(dz):
        return lax.rem(z + NZ - dz, NZ)

    def zn(dz):
        return lax.rem(z + dz, NZ)

    def xn(dx):
        return lax.rem(x + dx, NX)

    def yn(dy):
        return lax.rem(y + dy, NY)

    other_core = at(z, x, y, 1 - core)
    other_src = (1 - src, lat)
    other_x = at(z, 1 - x, y, core)

    def remote(src_ref, dst_ref, recv, device):
        return pltpu.make_async_remote_copy(
            src_ref=src_ref,
            dst_ref=dst_ref,
            send_sem=sent,
            recv_sem=recv,
            device_id=device,
            device_id_type=MESH,
        )

    def arrived(ref, recv):
        remote(ref, ref, recv, other_core).wait_recv()

    started = []

    def go(make, *args):
        make(*args).start()
        started.append((make, args))

    locals_ = [
        pltpu.make_async_copy(enc_hbm.at[0], enc.at[core], local_sem.at[0]),
        pltpu.make_async_copy(own_hbm.at[0], own_dec.at[core], local_sem.at[1]),
        pltpu.make_async_copy(cross_hbm, cross_dec.at[core], local_sem.at[2]),
        pltpu.make_async_copy(resid.at[0], row_buf, local_sem.at[3]),
        pltpu.make_async_copy(ids_hbm, ids_buf, local_sem.at[4]),
        pltpu.make_async_copy(bias, bias2.at[core], local_sem.at[5]),
        pltpu.make_async_copy(thresh, thresh2.at[core], local_sem.at[6]),
    ]
    for n in (3, 4, 5, 6, 0, 1, 2):
        locals_[n].start()

    barrier = pltpu.get_barrier_semaphore()
    peers = [at(zn(o), x, y, core) for o in range(1, NZ)]
    peers += [at(z, xn(dx), yn(dy), core) for dx, dy in PLANE_ORDER]
    peers += [other_core, other_src]
    for peer in peers:
        pl.semaphore_signal(barrier, inc=1, device_id=peer, device_id_type=MESH)

    locals_[3].wait()
    mine = row_buf[...].astype(F32)
    blocks[z, x, y] = jnp.concatenate(
        [mine[:, q * QUARTER : (q + 1) * QUARTER] for q in range(4)], axis=0
    ).astype(BF16)

    pl.semaphore_wait(barrier, len(peers))

    a_cols, z_cols = pl.ds(0, ZLAST), pl.ds(ZLAST, QUARTER - ZLAST)

    def b_cols(dz):
        return pl.ds(ZLAST, XFIRST[dz])

    def c_cols(dz):
        return pl.ds(ZLAST + XFIRST[dz], QUARTER - ZLAST - XFIRST[dz])

    def same(ref, recv, device):
        return remote(ref, ref, recv, device)

    def z_copy(o):
        ref = blocks.at[z, x, y, :, z_cols]
        return same(ref, z_recv.at[o], at(zn(o), x, y, core))

    def a1_copy(dx, dy):
        ref = blocks.at[z, x, y, :, a_cols]
        peer = at(z, xn(dx), yn(dy), core)
        return same(ref, a1_recv.at[0], peer)

    def az_copy(n):
        dz, o = ((0, 1), (0, 7), (0, 2), (0, 6), (2, 1), (6, 7), (2, 2), (6, 6))[n]
        xs = slice(None) if n < 6 else n - 6
        ref = blocks.at[zp(dz), xs, :, :, a_cols]
        return same(ref, az_recv.at[n], at(zn(o), x, y, core))

    AZ_OF = {1: (0,), 7: (1,), 2: (2,), 6: (3,), 3: (4,), 5: (5,), 4: (6, 7)}

    def cy_copy(dz, o):
        ref = blocks.at[zp(dz), x, y, :, c_cols(dz)]
        return same(ref, cy_recv.at[dz], at(z, x, yn(o), core))

    def bx_copy(dz):
        ref = blocks.at[zp(dz), x, y, :, b_cols(dz)]
        return same(ref, bx_recv.at[dz], other_x)

    def cx_copy(dz):
        ref = blocks.at[zp(dz), x, :, :, c_cols(dz)]
        return same(ref, cx_recv.at[dz], other_x)

    def by_copy(dz, o):
        ref = blocks.at[zp(dz), :, y, :, b_cols(dz)]
        return same(ref, by_recv.at[dz], at(z, x, yn(o), core))

    def second(dz):
        if dz:
            z_copy(dz).wait_recv()
        for o in Y_ORDER:
            go(cy_copy, dz, o)
        go(bx_copy, dz)

    def third(dz):
        bx_copy(dz).wait_recv()
        for o in Y_ORDER:
            go(by_copy, dz, o)
        arrived(blocks.at[zp(dz), x, pl.ds(0, 3), :, c_cols(dz)], cy_recv.at[dz])
        go(cx_copy, dz)

    def plane_done():
        arrived(blocks.at[pl.ds(0, 7), x, y, :, a_cols], a1_recv.at[0])
        for n in range(4):
            go(az_copy, n)

    def pass_on():
        for dz in (2, 6):
            for n in AZ_OF[dz]:
                az_copy(n).wait_recv()
            go(az_copy, 4 if dz == 2 else 5)
            go(az_copy, 6 if dz == 2 else 7)

    for o in Z_ORDER[1:]:
        go(z_copy, o)
    for dx, dy in PLANE_ORDER:
        go(a1_copy, dx, dy)
    second(0)

    def core_copy(n):
        src_ref, dst_ref = (
            (bias, bias2.at[core]),
            (thresh, thresh2.at[core]),
            (enc_hbm.at[0], enc.at[core]),
            (own_hbm.at[0], own_dec.at[core]),
            (cross_hbm, cross_dec.at[core]),
        )[n]
        return remote(src_ref, dst_ref, core_recv.at[n], other_core)

    for n in range(4):
        go(core_copy, n)

    @pl.when(src == 1)
    def _():
        core_copy(4).start()

    locals_[4].wait()
    shape = (2 * PLANE, 2 * PLANE)
    j = lax.broadcasted_iota(jnp.int32, shape, 0)
    plane, within = j // PLANE, j % PLANE
    step = within // (NX * NY * ROWS)
    far = jnp.where(step % 2 == 0, step // 2, NZ - (step + 1) // 2)
    pool = (z + far) % NZ * (NX * NY) + (within // ROWS) % (NX * NY)
    pool = pool * (2 * ROWS) + plane * ROWS + within % ROWS
    named = (jnp.broadcast_to(ids_buf[...], shape) == pool).astype(F32).astype(BF16)
    i = lax.broadcasted_iota(jnp.int32, shape, 0)
    t = lax.broadcasted_iota(jnp.int32, shape, 1)
    ir, iz, ixy = i % ROWS, (i // ROWS) % NZ, (i // (ROWS * NZ)) % (NX * NY)
    token = jnp.where(
        i < PLANE,
        (iz * NX * NY + ixy) * (2 * ROWS) + core * ROWS + ir,
        ((i - PLANE) // ROWS) * (2 * ROWS) + core * ROWS + ir,
    )
    order = (t == token).astype(F32).astype(BF16)
    select[...] = lax.dot_general(
        order, named, (((1,), (1,)), ((), ())), preferred_element_type=F32
    ).astype(BF16)

    second(1)
    second(7)
    plane_done()
    second(2)
    second(6)
    third(0)
    second(3)
    second(5)
    third(1)
    third(7)
    second(4)
    pass_on()
    third(2)
    third(6)
    third(3)
    third(5)
    third(4)

    def unpack(place, dz):
        zz = zp(dz)
        for xx in range(NX):
            four = [blocks[zz, xx, yy].astype(F32) for yy in range(NY)]
            start = (place * NX + xx) * (NY * ROWS)
            for q in range(4):
                rows[start : start + NY * ROWS, q * QUARTER : (q + 1) * QUARTER] = (
                    jnp.concatenate([b[4 * q : 4 * q + 4] for b in four], axis=0)
                ).astype(BF16)

    def bounds(c):
        first, end = PARTS[c]
        return first * NX * NY * ROWS, (end - first) * NX * NY * ROWS

    def code_copy(c):
        ref = codes.at[:, core, pl.ds(*bounds(c))]
        return same(ref, code_recv.at[0, c], other_core)

    def over_copy(c):
        return remote(
            codes.at[:, core, pl.ds(*bounds(c))],
            earlier.at[:, core, pl.ds(*bounds(c))],
            code_recv.at[1, c],
            other_src,
        )

    def on_copy(c):
        ref = earlier.at[:, core, pl.ds(*bounds(c))]
        return same(ref, code_recv.at[2, c], other_core)

    for c, (first, end) in enumerate(PARTS):
        for place in range(first, end):
            dz = Z_ORDER[place]
            for n in AZ_OF.get(dz, ()):
                if n not in AZ_OF[2] + AZ_OF[6]:
                    az_copy(n).wait_recv()
            arrived(blocks.at[zp(dz), :, pl.ds(0, 3), :, b_cols(dz)], by_recv.at[dz])
            cx_copy(dz).wait_recv()
            unpack(place, dz)
        if c == 0:
            for n in (0, 5, 6):
                locals_[n].wait()
            for n in range(3):
                core_copy(n).wait_recv()
        start, count = bounds(c)
        for h in range(2):
            pre = jnp.dot(
                rows[start : start + count], enc[h], preferred_element_type=F32
            )
            pre += bias2[h]
            gate = jnp.clip((pre - thresh2[h]) / 0.1, 0.0, 1.0)
            codes[h, core, start : start + count] = (pre * gate).astype(BF16)

        @pl.when(src == 0)
        def _():
            over_copy(c).start()

        go(code_copy, c)

    def permute(ref, into, h):
        into[:, h * LAT : (h + 1) * LAT] = jnp.dot(
            select[...], ref[h].reshape(2 * PLANE, LAT), preferred_element_type=F32
        ).astype(BF16)

    for c in range(len(PARTS)):
        code_copy(c).wait_recv()
    for h in range(2):
        permute(codes, mixed, h)
    locals_[1].wait()
    core_copy(3).wait_recv()
    locals_[2].wait()

    def product(left, right, n):
        start = PLANE if n < Z_TILES else 0
        return sum(
            jnp.dot(
                left[start : start + PLANE, h * LAT : (h + 1) * LAT],
                right[h, :, n * TILE : (n + 1) * TILE],
                preferred_element_type=F32,
            )
            for h in range(2)
        ).reshape(NX, NY, NZ * ROWS, TILE)

    def y1_copy(n, o):
        return remote(
            send1.at[n, :, yn(o)],
            got_y1.at[n, o],
            s1_recv.at[n],
            at(z, x, yn(o), core),
        )

    def x1_copy(n):
        return remote(
            send1.at[n, 1 - x], got_x1.at[n], s1_recv.at[n], other_x
        )

    def y2_copy(n, o):
        return remote(
            send2.at[n, yn(o)],
            got_y2.at[n, o],
            s2_recv.at[n],
            at(z, x, yn(o), core),
        )

    def x2_copy(n):
        return remote(
            send2.at[n, 1 - x], got_x2.at[n], s2_recv.at[n], other_x
        )

    def r1_copy(n, k):
        o, to, first, count = (
            (1, 1, 0, 32),
            (7, 7, 0, 32),
            (3, 1, 0, 32),
            (5, 7, 0, 32),
            (4, 2, 0, 16),
            (4, 6, 16, 16),
        )[k]
        zz = zn(o)
        return remote(
            send1.at[n, zz // NY, zz % NY, pl.ds(first, count)],
            got_a.at[n, k] if k < 4 else got_h.at[n, k - 4],
            r1_recv.at[n, k],
            at(zn(to), x, y, core),
        )

    def r2_copy(n, k):
        return remote(
            send2.at[n, k],
            got_a.at[n, 4 + k],
            r2_recv.at[n, k],
            at(zn((2, 6)[k]), x, y, core),
        )

    def last_copy(g, k):
        first, end = GROUPS[g]
        tiles = pl.ds(first, end - first)
        if first < Z_TILES:
            xx, yy = xn(k // NY), yn(k % NY)
            peer, place = at(z, xx, yy, core), xx * NY + yy
        else:
            peer, place = at(zn(k), x, y, core), zn(k)
        return remote(
            send3.at[place, tiles],
            got_z.at[k, tiles],
            s3_recv.at[g],
            peer,
        )

    def first_copies(n):
        if n < Z_TILES:
            return [(r1_copy, (n, k)) for k in (4, 5, 2, 3, 0, 1)]
        if n in Y_TILES:
            return [(y1_copy, (n, o)) for o in Y_ORDER]
        return [(x1_copy, (n,))]

    def stage1(n, total):
        send1[n] = total.astype(BF16)
        for make, args in first_copies(n):
            make(*args).start()

    def stage2(n):
        if n < Z_TILES:
            for k in (2, 3, 4, 5):
                r1_copy(n, k).wait_recv()
            for k in range(2):
                zz = zn((2, 6)[k])
                total = part[n, zz // NY, zz % NY] + got_a[n, 2 + k].astype(F32)
                more = got_h[n, k].astype(F32)
                top, low = total[:16], total[16:]
                if k == 0:
                    top += more
                else:
                    low += more
                send2[n, k, 0:16] = top.astype(BF16)
                send2[n, k, 16:32] = low.astype(BF16)
                go(r2_copy, n, k)
        elif n in Y_TILES:
            total = part[n, :, y]
            arrived(got_y1.at[n, pl.ds(1, 3)], s1_recv.at[n])
            for o in Y_ORDER:
                total += got_y1[n, o].astype(F32)
            half[n, 0:NX] = total
            send2[n, 0:NX] = total.astype(BF16)
            go(x2_copy, n)
        else:
            x1_copy(n).wait_recv()
            total = part[n, x] + got_x1[n].astype(F32)
            half[n] = total
            send2[n] = total.astype(BF16)
            for o in Y_ORDER:
                go(y2_copy, n, o)

    def stage3(n):
        if n < Z_TILES:
            total = part[n, z // NY, z % NY]
            for k in range(2):
                r1_copy(n, k).wait_recv()
                total += got_a[n, k].astype(F32)
            for k in range(2):
                r2_copy(n, k).wait_recv()
                total += got_a[n, 4 + k].astype(F32)
        elif n in Y_TILES:
            x2_copy(n).wait_recv()
            total = half[n, x] + got_x2[n].astype(F32)
        else:
            total = half[n, y]
            arrived(got_y2.at[n, pl.ds(1, 3)], s2_recv.at[n])
            for o in Y_ORDER:
                total += got_y2[n, o].astype(F32)
        step = TILE // 4
        for k in range(8):
            block = jnp.concatenate(
                [
                    total[k * ROWS : (k + 1) * ROWS, q * step : (q + 1) * step]
                    for q in range(4)
                ],
                axis=0,
            )
            last[k, n] = block
            send3[k, n] = block.astype(BF16)
        for g, (_, end) in enumerate(GROUPS):
            if n == end - 1:
                for k in (4, 3, 5, 2, 6, 1, 7):
                    go(last_copy, g, k)

    def finish(g):
        first, end = GROUPS[g]
        arrived(got_z.at[pl.ds(1, 7), pl.ds(first, end - first)], s3_recv.at[g])
        step = TILE // 4
        for n in range(first, end):
            total = last[x * NY + y if n < Z_TILES else z, n]
            for k in range(1, 8):
                total += got_z[k, n].astype(F32)
            for q in range(4):
                out[0, :, n * TILE + q * step : n * TILE + (q + 1) * step] = total[
                    q * ROWS : (q + 1) * ROWS
                ].astype(BF16)

    for n in TILE_ORDER:
        started.extend(first_copies(n))
        part[n] = product(mixed, own_dec, n)

        @pl.when(src == 0)
        def _():
            stage1(n, part[n])

    @pl.when(src == 1)
    def _():
        core_copy(4).wait_recv()
        for c in range(len(PARTS)):
            over_copy(c).wait_recv()
            on_copy(c).start()
        for c in range(len(PARTS)):
            on_copy(c).wait_recv()
        for h in range(2):
            permute(earlier, mixed_cross, h)
        for n in TILE_ORDER:
            total = part[n] + product(mixed_cross, cross_dec, n)
            part[n] = total
            stage1(n, total)

    for n in range(TILES + LAG):
        if n < TILES:
            stage2(n)
        if n >= LAG:
            stage3(n - LAG)
    for g in range(len(GROUPS)):
        finish(g)

    for make, args in started:
        make(*args).wait_send()

    @pl.when(src == 0)
    def _():
        for h in range(len(PARTS)):
            over_copy(h).wait_send()

    @pl.when(src == 1)
    def _():
        core_copy(4).wait_send()
        for h in range(len(PARTS)):
            on_copy(h).wait_send()


def on_device(
    resid, token_ids, enc_weight, enc_bias, threshold, dec_self, dec_cross
):
    vmem = pl.BlockSpec(memory_space=pltpu.VMEM)
    hbm = pl.BlockSpec(memory_space=pl.ANY)
    dma = pltpu.SemaphoreType.DMA
    scratch = [
        pltpu.VMEM((NZ, NX, NY, 16, QUARTER), BF16),
        pltpu.VMEM((PLANE, D), BF16),
        pltpu.VMEM((2, D, LAT), BF16),
        pltpu.VMEM((2, LAT, D), BF16),
        pltpu.VMEM((2, LAT, D), BF16),
        pltpu.VMEM((2, 1, LAT), F32),
        pltpu.VMEM((2, 1, LAT), F32),
        pltpu.VMEM((2, 2, PLANE, LAT), BF16),
        pltpu.VMEM((2, 2, PLANE, LAT), BF16),
        pltpu.VMEM((2 * PLANE, 2 * PLANE), BF16),
        pltpu.VMEM((2 * PLANE, 2 * LAT), BF16),
        pltpu.VMEM((2 * PLANE, 2 * LAT), BF16),
        pltpu.VMEM((TILES, NX, NY, NZ * ROWS, TILE), F32),
        pltpu.VMEM((TILES, NX, NY, NZ * ROWS, TILE), BF16),
        pltpu.VMEM((TILES, NY, NZ * ROWS, TILE), F32),
        pltpu.VMEM((TILES, NY, NZ * ROWS, TILE), BF16),
        pltpu.VMEM((NZ, TILES, 16, TILE // 4), BF16),
        pltpu.VMEM((NZ, TILES, 16, TILE // 4), F32),
        pltpu.VMEM((TILES, NY, NZ * ROWS, TILE), BF16),
        pltpu.VMEM((TILES, NY, NZ * ROWS, TILE), BF16),
        pltpu.VMEM((TILES, NY, NX, NZ * ROWS, TILE), BF16),
        pltpu.VMEM((TILES, NZ * ROWS, TILE), BF16),
        pltpu.VMEM((NZ, TILES, 16, TILE // 4), BF16),
        pltpu.VMEM((Z_TILES, 6, NZ * ROWS, TILE), BF16),
        pltpu.VMEM((Z_TILES, 2, 16, TILE), BF16),
        pltpu.VMEM((ROWS, D), BF16),
        pltpu.VMEM((1, 2 * PLANE), jnp.int32),
        dma((7,)),
        dma,
        dma((5,)),
        dma((3, len(PARTS))),
        dma((NZ,)),
        dma((NZ,)),
        dma((NZ,)),
        dma((NZ,)),
        dma((NZ,)),
        dma((1,)),
        dma((8,)),
        dma((Z_TILES, 6)),
        dma((Z_TILES, 2)),
        dma((TILES,)),
        dma((TILES,)),
        dma((len(GROUPS),)),
    ]
    return pl.pallas_call(
        kernel,
        out_shape=jax.ShapeDtypeStruct((1, ROWS, D), BF16),
        in_specs=[hbm] * 7,
        out_specs=vmem,
        scratch_shapes=scratch,
        compiler_params=pltpu.CompilerParams(
            collective_id=0, has_side_effects=True, vmem_limit_bytes=58 * 2**20
        ),
    )(
        token_ids.reshape(1, 2 * PLANE),
        resid,
        enc_bias,
        threshold,
        enc_weight,
        dec_self,
        dec_cross,
    )


def solution(mesh):
    in_specs = (
        P("src", "lat", None),
        P(),
        P("src", None, "lat"),
        P("src", "lat"),
        P("src", "lat"),
        P("src", "lat", None),
        P("lat", None),
    )
    out_specs = P("src", "lat", None)
    return jax.shard_map(
        on_device, mesh=mesh, in_specs=in_specs, out_specs=out_specs, check_vma=False
    )
```
